32 devices in a mesh: section: 4 (over y, x), ctx: 8 (over z, core).
Axes of the slice: x: 2, y: 2, z: 4, core: 2. Of those that a mesh axis runs over, the one named last changes fastest.
Arguments:
- queries: bfloat16 [4, 3072, 40, 128], P('section', 'ctx'), may hold values from -60 to 60
- keys_values: bfloat16 [3072, 2, 40, 128], P('ctx', None, 'section'), may hold values from -6 to 6
- positions: int32 [3072], P('ctx'), may hold values from 0 to 1533, as said below
- documents: int32 [3072], P('ctx'), may hold values from 0 to 3071, as said below
Outputs:
- attended: bfloat16 [4, 3072, 40, 128], P('section', 'ctx')
The draws below stay inside these ranges and needn't reach their ends.
Inputs may be any that keep to these rules, and one draw needn't show every extreme that they name: `documents`: Non-decreasing along the sequence; each document is a run of 1 to 384 tokens sharing one id, one document has exactly 384 tokens, and the last document's id is 3071. `positions`: within a document the ids rise by 1 to 3 from each token to the next; a document's first id is 0 to 384.
All inputs are finite; a program needn't handle non-finite values.
Results may differ from the reference program's by a relative error of at most 0.01.
Values may be sent and summed in bfloat16 or wider, within the bound.
No kernel may reach another device: no remote copies, remote signals or barrier semaphores. Data moves between devices by JAX's collectives and lax.ppermute only.
A program may use at most 128 MiB of HBM per device.

```python
import jax
import jax.numpy as jnp
from jax import lax

HEADS = 40
HEAD_DIM = 128
TOK_DEV = 384
SECTIONS = 4
TOKENS = 3072


def doc_layout(key):
    length_key, offset_key, step_key = jax.random.split(jax.random.fold_in(key, 7), 3)
    lengths = jax.random.randint(length_key, (TOKENS,), 1, TOK_DEV + 1)
    doc_index = jnp.arange(TOKENS)
    lengths = jnp.where(doc_index == 0, TOK_DEV // 2, lengths)
    lengths = jnp.where(doc_index == 1, TOK_DEV, lengths).astype(jnp.int32)
    endings = jnp.cumsum(lengths)
    starting = endings - lengths
    token_index = jnp.arange(TOKENS, dtype=jnp.int32)
    doc_ids = (jnp.searchsorted(starting, token_index, side='right') - 1).astype(jnp.int32)
    strides = jax.random.randint(step_key, (TOKENS,), 1, 4).astype(jnp.int32)
    strides = jnp.where(doc_ids == 1, 3, strides).astype(jnp.int32)
    running = jnp.cumsum(strides).astype(jnp.int32)
    offsets = jax.random.randint(offset_key, (TOKENS,), 0, TOK_DEV + 1).astype(jnp.int32)
    offsets = jnp.where(doc_index == 0, 0, offsets)
    offsets = jnp.where(doc_index == 1, TOK_DEV, offsets).astype(jnp.int32)
    first_token = starting[doc_ids]
    position_ids = running - running[first_token] + offsets[doc_ids]
    last_doc = doc_ids[TOKENS - 1]
    doc_ids = jnp.where(doc_ids == last_doc, TOKENS - 1, doc_ids).astype(jnp.int32)
    return (doc_ids, position_ids.astype(jnp.int32))


def draw_documents(key, part):
    return doc_layout(key)[0]


def draw_positions(key, part):
    return doc_layout(key)[1]


def kv_base(key):
    kv_key = jax.random.fold_in(key, 11)
    array_shape = (TOKENS, 2, HEADS, HEAD_DIM)
    drawn = jnp.clip(jax.random.normal(kv_key, array_shape, jnp.float32), -6.0, 6.0)
    return drawn


def draw_keys_values(key, part):
    return kv_base(key).astype(jnp.bfloat16)


def draw_queries(key, part):
    array_shape = (SECTIONS, TOKENS, HEADS, HEAD_DIM)
    query_key = jax.random.fold_in(key, 13)
    drawn = jnp.clip(jax.random.normal(query_key, array_shape, jnp.float32), -6.0, 6.0)
    return drawn.astype(jnp.bfloat16)


def setup_inputs(seed: int = 0) -> dict:
    arg_keys = jax.random.split(jax.random.key(seed), 5)
    return {
        "queries": draw_queries(jax.random.fold_in(arg_keys[4], 71), 0),
        "keys_values": draw_keys_values(jax.random.fold_in(arg_keys[4], 71), 0),
        "positions": draw_positions(jax.random.fold_in(arg_keys[4], 71), 0),
        "documents": draw_documents(jax.random.fold_in(arg_keys[4], 71), 0),
    }


def rotate(values, token_positions):
    half_dim = values.shape[-1] // 2
    exponent = jnp.arange(half_dim, dtype=jnp.float32) * (2.0 / values.shape[-1])
    inverse = jnp.power(jnp.float32(10000.0), -exponent)
    angles = token_positions.astype(jnp.float32)[:, None] * inverse[None, :]
    cosine = jnp.cos(angles)[:, None, :]
    sine = jnp.sin(angles)[:, None, :]
    widened = values.astype(jnp.float32)
    lower = widened[..., :half_dim]
    upper = widened[..., half_dim:]
    joined = jnp.concatenate([lower * cosine - upper * sine, upper * cosine + lower * sine], axis=-1)
    return joined.astype(jnp.bfloat16)


def reference(queries, keys_values, positions, documents):
    rotated = rotate(queries, positions)
    cache_keys = rotate(keys_values[:, 0], positions)
    cache_values = keys_values[:, 1]
    padded_keys = jnp.concatenate([jnp.zeros((TOK_DEV, HEADS, HEAD_DIM), jnp.bfloat16), cache_keys], axis=0)
    padded_values = jnp.concatenate([jnp.zeros((TOK_DEV, HEADS, HEAD_DIM), jnp.bfloat16), cache_values], axis=0)
    padded_docs = jnp.concatenate([jnp.full((TOK_DEV,), -1, jnp.int32), documents.astype(jnp.int32)], axis=0)
    block_count = TOKENS // TOK_DEV
    scale = HEAD_DIM ** -0.5
    zero_index = jnp.zeros((), jnp.int32)
    causal = jnp.arange(2 * TOK_DEV)[None, :] <= jnp.arange(TOK_DEV)[:, None] + TOK_DEV

    def one_block(pair_index):
        section_index = (pair_index // block_count).astype(jnp.int32)
        row_start = ((pair_index % block_count) * TOK_DEV).astype(jnp.int32)
        query_block = lax.dynamic_slice(rotated, (section_index, row_start, zero_index, zero_index), (1, TOK_DEV, HEADS, HEAD_DIM))[0]
        key_block = lax.dynamic_slice_in_dim(padded_keys, row_start, 2 * TOK_DEV, 0)
        value_block = lax.dynamic_slice_in_dim(padded_values, row_start, 2 * TOK_DEV, 0)
        key_docs = lax.dynamic_slice_in_dim(padded_docs, row_start, 2 * TOK_DEV, 0)
        query_docs = lax.dynamic_slice_in_dim(documents.astype(jnp.int32), row_start, TOK_DEV, 0)
        allowed = jnp.logical_and(key_docs[None, :] == query_docs[:, None], causal)
        scores = jnp.einsum("qhd,khd->hqk", query_block.astype(jnp.float32), key_block.astype(jnp.float32)) * scale
        scores = jnp.where(allowed[None], scores, -1e30)
        largest = jnp.max(scores, axis=-1, keepdims=True)
        weights = jnp.exp(scores - largest)
        probs = (weights / jnp.sum(weights, axis=-1, keepdims=True)).astype(jnp.bfloat16)
        mixed = jnp.einsum("hqk,khd->qhd", probs.astype(jnp.float32), value_block.astype(jnp.float32))
        return mixed.astype(jnp.bfloat16)

    blocks_out = lax.map(one_block, jnp.arange(SECTIONS * block_count, dtype=jnp.int32))
    return blocks_out.reshape(SECTIONS, TOKENS, HEADS, HEAD_DIM)
```

```python
import functools

import jax
import jax.numpy as jnp
import numpy as np
from jax import lax
from jax.experimental import pallas as pl
from jax.experimental.pallas import tpu as pltpu
from jax.sharding import PartitionSpec as P

ACROSS_X = ((0, 1), (1, 0), (2, 3), (3, 2))
ACROSS_Y = ((0, 2), (2, 0), (1, 3), (3, 1))
BLOCK = 128
PARAMS = pltpu.CompilerParams(vmem_limit_bytes=48 * 2**20)
NT = (((1,), (1,)), ((), ()))


def shifted(block, axis, distance):
    devices = range(lax.axis_size(axis))
    route = [(i - distance, i) for i in devices if i - distance in devices]
    return lax.ppermute(block, axis, route)


def angle_tables(token_positions, head_dim):
    half_dim = head_dim // 2
    exponent = jnp.arange(half_dim, dtype=jnp.float32) * (2.0 / head_dim)
    inverse = jnp.power(jnp.float32(10000.0), -exponent)
    angles = token_positions.astype(jnp.float32)[:, None] * inverse[None, :]
    cosine = jnp.cos(angles)
    sine = jnp.sin(angles)
    return jnp.concatenate([cosine, cosine], axis=1), jnp.concatenate([-sine, sine], axis=1)


def turn(values, cosine, sine):
    return (values * cosine + pltpu.roll(values, values.shape[-1] // 2, 1) * sine).astype(jnp.bfloat16)


def prepare_cache(keys_values, cosine, sine):
    tokens, _, heads, head_dim = keys_values.shape
    half = heads // 2
    step = BLOCK
    rows = jnp.transpose(keys_values, (0, 2, 1, 3)).reshape(tokens * heads * 2, head_dim)

    def kernel(rows_ref, cosine_ref, sine_ref, all_ref, a_ref, b_ref, wide):
        wide[...] = rows_ref[...].astype(jnp.float32)
        for head in range(heads):
            key = wide[pl.ds(2 * head, step, stride=2 * heads), :]
            key = turn(key, cosine_ref[...], sine_ref[...])
            value = wide[pl.ds(2 * head + 1, step, stride=2 * heads), :].astype(jnp.bfloat16)
            part = a_ref if head < half else b_ref
            all_ref[0, head] = key
            all_ref[1, head] = value
            part[0, head % half] = key
            part[1, head % half] = value

    table = pl.BlockSpec((step, head_dim), lambda i: (i, 0))
    counts = (heads, half, heads - half)
    return pl.pallas_call(
        kernel,
        grid=(tokens // step,),
        in_specs=[pl.BlockSpec((step * heads * 2, head_dim), lambda i: (i, 0)), table, table],
        out_specs=[pl.BlockSpec((2, n, step, head_dim), lambda i: (0, 0, i, 0)) for n in counts],
        out_shape=[jax.ShapeDtypeStruct((2, n, tokens, head_dim), jnp.bfloat16) for n in counts],
        scratch_shapes=[pltpu.VMEM((step * heads * 2, head_dim), jnp.float32)],
        compiler_params=PARAMS,
        name="prepare_cache",
    )(rows, cosine, sine)


def prepare_queries(queries, cosine, sine, starts, counts):
    tokens, heads, head_dim = queries.shape
    step = BLOCK

    def kernel(starts_ref, queries_ref, cosine_ref, sine_ref, *refs):
        wide = refs[-1]
        wide[...] = queries_ref[...].reshape(step * heads, head_dim).astype(jnp.float32)
        run = 0
        for out_ref, runs in zip(refs[:-1], counts):
            slot = 0
            for count in runs:
                for i in range(count):
                    head = wide[pl.ds(starts_ref[run] + i, step, stride=heads), :]
                    out_ref[slot] = turn(head, cosine_ref[...], sine_ref[...])
                    slot += 1
                run += 1

    table = pl.BlockSpec((step, head_dim), lambda i, s: (i, 0))
    totals = [sum(runs) for runs in counts]
    return pl.pallas_call(
        kernel,
        grid_spec=pltpu.PrefetchScalarGridSpec(
            num_scalar_prefetch=1,
            grid=(tokens // step,),
            in_specs=[pl.BlockSpec((step, heads, head_dim), lambda i, s: (i, 0, 0)), table, table],
            out_specs=[pl.BlockSpec((n, step, head_dim), lambda i, s: (0, i, 0)) for n in totals],
            scratch_shapes=[pltpu.VMEM((step * heads, head_dim), jnp.float32)],
        ),
        out_shape=[jax.ShapeDtypeStruct((n, tokens, head_dim), jnp.bfloat16) for n in totals],
        compiler_params=PARAMS,
        name="prepare_queries",
    )(starts, queries, cosine, sine)


def mask_bias(documents, earlier_docs):
    tokens = documents.shape[0]
    window = jnp.concatenate([earlier_docs, documents])
    blocks = tokens // BLOCK
    width = tokens + BLOCK
    keys = jnp.stack([window[BLOCK * r : BLOCK * r + width] for r in range(blocks)])
    rows = documents.reshape(blocks, BLOCK)
    causal = jnp.arange(width)[None, :] <= jnp.arange(BLOCK)[:, None] + tokens
    allowed = jnp.logical_and(keys[:, None, :] == rows[:, :, None], causal[None])
    return jnp.where(allowed, 0.0, -1e30).astype(jnp.float32)


def attend(queries, current, earlier, bias):
    count = queries[0][2]
    tokens, head_dim = queries[0][0].shape[-2:]
    blocks = tokens // BLOCK
    scale = float(head_dim**-0.5 * np.log2(np.e))

    def kernel(qa, qb, ca, cb, ea, eb, bias_ref, oa, ob):
        for q, c, e, o in ((qa, ca, ea, oa), (qb, cb, eb, ob)):
            for r in range(blocks):
                low, high = BLOCK * r, BLOCK * (r + 1)
                key = jnp.concatenate([e[0, 0, low:], c[0, 0, :high]], axis=0)
                value = jnp.concatenate([e[1, 0, low:], c[1, 0, :high]], axis=0)
                scores = lax.dot_general(q[0, low:high], key, NT, preferred_element_type=jnp.float32)
                scores = scores + bias_ref[r]
                largest = jnp.max(scores, axis=1, keepdims=True) * scale
                weights = jnp.exp2(scores * scale - largest).astype(jnp.bfloat16)
                extended = jnp.concatenate([value, jnp.ones_like(value)], axis=1)
                mixed = jnp.dot(weights, extended, preferred_element_type=jnp.float32)
                o[0, low:high] = (mixed[:, :head_dim] / mixed[:, head_dim:]).astype(jnp.bfloat16)

    def one(first):
        return pl.BlockSpec((1, tokens, head_dim), lambda i: (i + first, 0, 0))

    def pair(first):
        return pl.BlockSpec((2, 1, tokens, head_dim), lambda i: (0, i + first, 0, 0))

    operands = [*queries, *current, *earlier]
    in_specs = [one(o[1]) for o in queries] + [pair(o[1]) for o in (*current, *earlier)]
    in_specs.append(pl.BlockSpec(bias.shape, lambda i: (0, 0, 0)))
    return pl.pallas_call(
        kernel,
        grid=(count,),
        in_specs=in_specs,
        out_specs=[one(0)] * 2,
        out_shape=[jax.ShapeDtypeStruct((count, tokens, head_dim), jnp.bfloat16)] * 2,
        compiler_params=PARAMS,
        cost_estimate=pl.CostEstimate(
            flops=2 * count * 2 * blocks * BLOCK * (tokens + BLOCK) * head_dim * 2,
            bytes_accessed=2 * count * 6 * tokens * head_dim * 2,
            transcendentals=2 * count * blocks * BLOCK * (tokens + BLOCK),
        ),
        name="attend",
    )(*[o[0] for o in operands], bias)


def assemble(pieces, slots):
    count, tokens, head_dim = pieces[0].shape
    heads = count * len(pieces)
    step = BLOCK

    def kernel(slots_ref, *refs):
        *piece_refs, out_ref, gathered = refs
        for p, ref in enumerate(piece_refs):
            gathered[pl.ds(slots_ref[p] * count, count)] = ref[...]
        out_ref[...] = jnp.swapaxes(gathered[...], 0, 1)

    return pl.pallas_call(
        kernel,
        grid_spec=pltpu.PrefetchScalarGridSpec(
            num_scalar_prefetch=1,
            grid=(tokens // step,),
            in_specs=[pl.BlockSpec((count, step, head_dim), lambda i, s: (0, i, 0))] * len(pieces),
            out_specs=pl.BlockSpec((step, heads, head_dim), lambda i, s: (i, 0, 0)),
            scratch_shapes=[pltpu.VMEM((heads, step, head_dim), jnp.bfloat16)],
        ),
        out_shape=jax.ShapeDtypeStruct((tokens, heads, head_dim), jnp.bfloat16),
        compiler_params=PARAMS,
        name="assemble",
    )(slots, *pieces)


def across(value, route):
    return lax.ppermute(value, "section", route)


def square_body(queries, keys_values, positions, documents):
    head_dim = queries.shape[-1]
    mine = keys_values.shape[2]
    half = mine // 2
    section = lax.axis_index("section")
    beside_x, beside_y, opposite = section ^ 1, section ^ 2, section ^ 3
    earlier_docs = shifted(documents, "ctx", 1)
    earlier_docs = jnp.where(lax.axis_index("ctx") == 0, -1, earlier_docs)

    cosine, sine = angle_tables(positions, head_dim)
    share, share_a, share_b = prepare_cache(keys_values, cosine, sine)
    cache_a = across(share_a, ACROSS_X)
    cache_b = across(share_b, ACROSS_Y)
    earlier = shifted(share, "ctx", 1)

    starts = jnp.stack(
        [
            beside_y * mine,
            beside_x * mine + half,
            opposite * mine,
            opposite * mine + half,
            section * mine,
            beside_x * mine,
            beside_y * mine + half,
        ]
    ).astype(jnp.int32)
    near_y, near_x, far_y, far_x, own_near, own_far = prepare_queries(
        queries[0], cosine, sine, starts, ((half,), (half,), (half,), (half,), (mine,), (half, half))
    )
    bias = mask_bias(documents, earlier_docs)
    near_a = across(near_y, ACROSS_Y)
    near_b = across(near_x, ACROSS_X)
    far_a = across(far_y, ACROSS_Y)
    far_b = across(far_x, ACROSS_X)
    earlier_a = shifted(cache_a, "ctx", 1)
    earlier_b = shifted(cache_b, "ctx", 1)

    near_cache = ((share, 0), (share, half))
    near_earlier = ((earlier, 0), (earlier, half))
    far_cache = ((cache_a, 0), (cache_b, 0))
    far_earlier = ((earlier_a, 0), (earlier_b, 0))
    out_near_a, out_near_b = attend(((near_a, 0, half), (near_b, 0, half)), near_cache, near_earlier, bias)
    back_near_a = across(out_near_a, ACROSS_Y)
    back_near_b = across(out_near_b, ACROSS_X)
    out_far_a, out_far_b = attend(((far_a, 0, half), (far_b, 0, half)), far_cache, far_earlier, bias)
    back_far_a = across(out_far_a, ACROSS_Y)
    back_far_b = across(out_far_b, ACROSS_X)
    own_near_a, own_near_b = attend(((own_near, 0, half), (own_near, half, half)), near_cache, near_earlier, bias)
    own_far_a, own_far_b = attend(((own_far, 0, half), (own_far, half, half)), far_cache, far_earlier, bias)

    slots = jnp.stack(
        [
            2 * section,
            2 * section + 1,
            2 * beside_x,
            2 * beside_y + 1,
            2 * beside_y,
            2 * beside_x + 1,
            2 * opposite,
            2 * opposite + 1,
        ]
    ).astype(jnp.int32)
    pieces = (own_near_a, own_near_b, own_far_a, own_far_b, back_near_a, back_near_b, back_far_a, back_far_b)
    return assemble(pieces, slots)[None]


def general_body(queries, keys_values, positions, documents):
    tokens, heads, head_dim = queries.shape[1:]
    mine = keys_values.shape[2]
    cosine, sine = angle_tables(positions, head_dim)
    earlier_docs = shifted(documents, "ctx", 1)
    earlier_docs = jnp.where(lax.axis_index("ctx") == 0, -1, earlier_docs)
    share = prepare_cache(keys_values, cosine, sine)[0]
    whole = lax.all_gather(share, "section", axis=1, tiled=True)
    earlier = shifted(whole, "ctx", 1)
    starts = jnp.zeros((1,), jnp.int32)
    (rotated,) = prepare_queries(queries[0], cosine, sine, starts, ((heads,),))
    bias = mask_bias(documents, earlier_docs)
    half = heads // 2
    outs = attend(
        ((rotated, 0, half), (rotated, half, half)),
        ((whole, 0), (whole, half)),
        ((earlier, 0), (earlier, half)),
        bias,
    )
    return assemble(outs, jnp.arange(2, dtype=jnp.int32))[None]


def solution(mesh):
    placed = (P("section", "ctx", None, None), P("ctx", None, "section", None), P("ctx"), P("ctx"))
    body = square_body if mesh.shape["section"] == 4 else general_body
    return jax.shard_map(
        body, mesh=mesh, in_specs=placed, out_specs=P("section", "ctx", None, None), check_vma=False
    )
```

```python
import functools

import jax
import jax.numpy as jnp
import numpy as np
from jax import lax
from jax.experimental import pallas as pl
from jax.experimental.pallas import tpu as pltpu
from jax.sharding import PartitionSpec as P

ACROSS_X = ((0, 1), (1, 0), (2, 3), (3, 2))
ACROSS_Y = ((0, 2), (2, 0), (1, 3), (3, 1))
BLOCK = 128
ROWS = 8
ID_BASE = 256
ID_ROWS = 16
PARAMS = pltpu.CompilerParams(vmem_limit_bytes=12 * 2**20)
IN_VMEM = pl.BlockSpec(memory_space=pltpu.VMEM)
IN_SMEM = pl.BlockSpec(memory_space=pltpu.SMEM)
NT = (((1,), (1,)), ((), ()))


def shifted(block, axis):
    size = lax.axis_size(axis)
    return lax.ppermute(block, axis, [(i, (i + 1) % size) for i in range(size)])


def turn(values, cosine, sine):
    return (values * cosine + pltpu.roll(values, values.shape[-1] // 2, 1) * sine).astype(jnp.bfloat16)


def prepare_cache(keys_values, positions, documents):
    tokens, _, heads, head_dim = keys_values.shape
    half = heads // 2
    half_dim = head_dim // 2
    steps = tokens // BLOCK
    chunk = BLOCK * heads * 2
    rows = jnp.transpose(keys_values, (0, 2, 1, 3)).reshape(tokens * heads * 2, head_dim)
    exponent = np.arange(half_dim, dtype=np.float32) * np.float32(2.0 / head_dim)
    inverse = np.power(np.float32(10000.0), -exponent).astype(np.float32)
    inverse = jnp.asarray(np.concatenate([inverse, inverse])[None])

    def kernel(positions_hbm, documents_hbm, inverse_hbm, rows_ref, all_ref, a_ref, b_ref, cosine_ref, sine_ref, *scratch):
        positions_ref, documents_ref, inverse_ref, ids, landed, wide, done, small_sems, row_sems, store_sems = scratch
        small = [
            pltpu.make_async_copy(positions_hbm, positions_ref, small_sems.at[0]),
            pltpu.make_async_copy(documents_hbm, documents_ref, small_sems.at[1]),
            pltpu.make_async_copy(inverse_hbm, inverse_ref, small_sems.at[2]),
        ]
        copies = [
            pltpu.make_async_copy(rows_ref.at[pl.ds(i * chunk, chunk)], landed.at[i], row_sems.at[i])
            for i in range(steps)
        ]
        for copy in (*small, *copies):
            copy.start()
        for copy in small:
            copy.wait()
        left = lax.broadcasted_iota(jnp.int32, (BLOCK, head_dim), 1) < half_dim
        columns = [
            jnp.transpose(jnp.broadcast_to(positions_ref[i : i + 1], (BLOCK, BLOCK))).astype(jnp.float32)
            for i in range(steps)
        ]
        for i in range(0, steps, 2):
            other = min(i + 1, steps - 1)
            angles = jnp.where(left, columns[i], columns[other]) * inverse_ref[...]
            cosine, sine = jnp.cos(angles), jnp.sin(angles)
            turned_cosine, turned_sine = (pltpu.roll(t, half_dim, 1) for t in (cosine, sine))
            for k, (c, s) in enumerate(
                (
                    (jnp.where(left, cosine, turned_cosine), jnp.where(left, -sine, turned_sine)),
                    (jnp.where(left, turned_cosine, cosine), jnp.where(left, -turned_sine, sine)),
                )
            ):
                if i + k < steps:
                    at = slice((i + k) * BLOCK, (i + k + 1) * BLOCK)
                    cosine_ref[at] = c
                    sine_ref[at] = s
        ids[...] = jnp.concatenate(
            [
                documents_ref[...] // ID_BASE,
                documents_ref[...] % ID_BASE,
                jnp.zeros((ID_ROWS - 2 * steps, BLOCK), jnp.int32),
            ],
            axis=0,
        ).astype(jnp.float32).astype(jnp.bfloat16)
        stores = [
            pltpu.make_async_copy(ids, all_ref.at[2 * heads, pl.ds(0, ID_ROWS)], store_sems.at[0])
        ]
        stores[0].start()
        for i in range(steps):
            at = slice(i * BLOCK, (i + 1) * BLOCK)
            copies[i].wait()
            wide[...] = landed[i].astype(jnp.float32)
            for head in range(heads):
                key = wide[pl.ds(2 * head, BLOCK, stride=2 * heads), :]
                done[i, head] = turn(key, cosine_ref[at], sine_ref[at])
                done[i, heads + head] = wide[pl.ds(2 * head + 1, BLOCK, stride=2 * heads), :].astype(jnp.bfloat16)
            rows_at = pl.ds(i * BLOCK, BLOCK)
            moves = [(done.at[i], all_ref.at[pl.ds(0, 2 * heads), rows_at])]
            for k in range(2):
                moves.append((done.at[i, pl.ds(k * heads, half)], a_ref.at[k, :, rows_at]))
                moves.append((done.at[i, pl.ds(k * heads + half, heads - half)], b_ref.at[k, :, rows_at]))
            for source, target in moves:
                store = pltpu.make_async_copy(source, target, store_sems.at[len(stores)])
                store.start()
                stores.append(store)
        for store in stores:
            store.wait()

    table = jax.ShapeDtypeStruct((tokens, head_dim), jnp.float32)
    anywhere = pl.BlockSpec(memory_space=pl.ANY)
    return pl.pallas_call(
        kernel,
        in_specs=[anywhere] * 4,
        out_specs=[anywhere] * 3 + [IN_VMEM] * 2,
        out_shape=[
            jax.ShapeDtypeStruct((2 * heads + 1, tokens, head_dim), jnp.bfloat16),
            *(jax.ShapeDtypeStruct((2, n, tokens, head_dim), jnp.bfloat16) for n in (half, heads - half)),
            table,
            table,
        ],
        scratch_shapes=[
            pltpu.VMEM((steps, BLOCK), jnp.int32),
            pltpu.VMEM((steps, BLOCK), jnp.int32),
            pltpu.VMEM((1, head_dim), jnp.float32),
            pltpu.VMEM((ID_ROWS, BLOCK), jnp.bfloat16),
            pltpu.VMEM((steps, chunk, head_dim), jnp.bfloat16),
            pltpu.VMEM((chunk, head_dim), jnp.float32),
            pltpu.VMEM((steps, 2 * heads, BLOCK, head_dim), jnp.bfloat16),
            pltpu.SemaphoreType.DMA((3,)),
            pltpu.SemaphoreType.DMA((steps,)),
            pltpu.SemaphoreType.DMA((1 + 5 * steps,)),
        ],
        compiler_params=pltpu.CompilerParams(vmem_limit_bytes=60 * 2**20),
        name="prepare_cache",
    )(positions.reshape(steps, BLOCK), documents.reshape(steps, BLOCK), inverse, rows)


def prepare_queries(queries, cosine, sine, starts, counts):
    tokens, heads, head_dim = queries.shape

    def kernel(starts_ref, queries_ref, cosine_ref, sine_ref, *refs):
        wide = refs[-1]
        wide[...] = queries_ref[...].reshape(tokens * heads, head_dim).astype(jnp.float32)
        run = 0
        for out_ref, runs in zip(refs[:-1], counts):
            slot = 0
            for count in runs:
                for i in range(count):
                    head = wide[pl.ds(starts_ref[run] + i, tokens, stride=heads), :]
                    out_ref[slot] = turn(head, cosine_ref[...], sine_ref[...])
                    slot += 1
                run += 1

    totals = [sum(runs) for runs in counts]
    return pl.pallas_call(
        kernel,
        in_specs=[IN_SMEM] + [IN_VMEM] * 3,
        out_specs=[IN_VMEM] * len(totals),
        out_shape=[jax.ShapeDtypeStruct((n, tokens, head_dim), jnp.bfloat16) for n in totals],
        scratch_shapes=[pltpu.VMEM((tokens * heads, head_dim), jnp.float32)],
        compiler_params=PARAMS,
        cost_estimate=pl.CostEstimate(
            flops=2 * 10**9, bytes_accessed=4 * queries.size, transcendentals=0
        ),
        name="prepare_queries",
    )(starts, queries, cosine, sine)


def attend(sets, documents, earlier_docs, flops=1):
    count = sets[0][0][2]
    tokens, head_dim = sets[0][0][0].shape[-2:]
    blocks = tokens // BLOCK
    width = tokens + BLOCK
    scale = float(head_dim**-0.5 * np.log2(np.e))
    n = len(sets)

    def kernel(docs_ref, earlier_ref, *refs):
        bias = refs[-1]
        window = [earlier_ref[i : i + 1] for i in range(blocks)] + [docs_ref[i : i + 1] for i in range(blocks)]
        row = lax.broadcasted_iota(jnp.int32, (BLOCK, BLOCK), 0)
        column = lax.broadcasted_iota(jnp.int32, (BLOCK, BLOCK), 1)
        for r in range(blocks):
            mine = jnp.transpose(jnp.broadcast_to(docs_ref[r : r + 1], (BLOCK, BLOCK)))
            for c in range(blocks + 1):
                allowed = window[r + c] == mine
                if c == blocks:
                    allowed = jnp.logical_and(allowed, column <= row)
                bias[r, :, c * BLOCK : (c + 1) * BLOCK] = jnp.where(allowed, 0.0, -1e30)
        for head in range(count):
            for g, group in enumerate(sets):
                q, c, e = refs[3 * g : 3 * g + 3]
                q_head = group[0][1] + head

                def band(kind, low, high):
                    (_, c_first, c_heads), (_, e_first, e_heads) = group[1:]
                    c_row = (kind * c_heads + c_first + head) * tokens
                    e_row = (kind * e_heads + e_first + head) * tokens
                    return jnp.concatenate([e[e_row + low : e_row + tokens], c[c_row : c_row + high]], axis=0)

                for r in range(blocks):
                    low, high = BLOCK * r, BLOCK * (r + 1)
                    key, value = band(0, low, high), band(1, low, high)
                    scores = lax.dot_general(q[q_head, low:high], key, NT, preferred_element_type=jnp.float32)
                    scores = scores + bias[r]
                    largest = jnp.max(scores, axis=1, keepdims=True) * scale
                    weights = jnp.exp2(scores * scale - largest).astype(jnp.bfloat16)
                    extended = jnp.concatenate([value, jnp.ones_like(value)], axis=1)
                    mixed = jnp.dot(weights, extended, preferred_element_type=jnp.float32)
                    mixed = (mixed[:, :head_dim] / mixed[:, head_dim:]).astype(jnp.bfloat16)
                    refs[3 * n + g][head, low:high] = mixed

    return pl.pallas_call(
        kernel,
        in_specs=[IN_VMEM] * (2 + 3 * n),
        out_specs=[IN_VMEM] * n,
        out_shape=[jax.ShapeDtypeStruct((count, tokens, head_dim), jnp.bfloat16)] * n,
        scratch_shapes=[pltpu.VMEM((blocks, BLOCK, width), jnp.float32)],
        compiler_params=PARAMS,
        cost_estimate=pl.CostEstimate(flops=flops, bytes_accessed=1, transcendentals=0),
        name="attend",
    )(documents.reshape(blocks, BLOCK), earlier_docs.reshape(blocks, BLOCK), *[o[0] for group in sets for o in group])


def assemble(pieces, slots, heads, window_start=None, window=0):
    count, tokens, head_dim = pieces[0].shape
    step = BLOCK

    def kernel(slots_ref, *refs):
        piece_refs, outs, gathered = refs[: len(pieces)], refs[len(pieces) : -1], refs[-1]
        for p, ref in enumerate(piece_refs):
            gathered[pl.ds(slots_ref[p] * count, count)] = ref[...]
        outs[0][...] = jnp.swapaxes(gathered[...], 0, 1)
        if window:
            first = pl.multiple_of(slots_ref[len(pieces)] * ROWS, ROWS)
            outs[1][...] = jnp.swapaxes(gathered[pl.ds(first, window)], 0, 1)

    if window:
        slots = jnp.concatenate([slots, window_start[None]])
    counts = (heads, window) if window else (heads,)
    return pl.pallas_call(
        kernel,
        grid_spec=pltpu.PrefetchScalarGridSpec(
            num_scalar_prefetch=1,
            grid=(tokens // step,),
            in_specs=[pl.BlockSpec((count, step, head_dim), lambda i, s: (0, i, 0))] * len(pieces),
            out_specs=[pl.BlockSpec((step, n, head_dim), lambda i, s: (i, 0, 0)) for n in counts],
            scratch_shapes=[pltpu.VMEM((heads, step, head_dim), jnp.bfloat16)],
        ),
        out_shape=[jax.ShapeDtypeStruct((tokens, n, head_dim), jnp.bfloat16) for n in counts],
        compiler_params=PARAMS,
        cost_estimate=pl.CostEstimate(flops=10**9, bytes_accessed=1, transcendentals=0),
        name="assemble",
    )(slots, *pieces)


def complete(gathered, old, pieces, slot):
    count, tokens, head_dim = pieces[0].shape
    mine = 2 * count
    window = old.shape[1]

    def kernel(slot_ref, first_ref, second_ref, old_ref, _, out_ref, placed):
        j = pl.program_id(0)
        block = (slot_ref[0] * mine) // ROWS
        low = slot_ref[0] * mine - block * ROWS

        @pl.when(j == 0)
        def _():
            placed[pl.ds(low, count)] = first_ref[...]
            placed[pl.ds(low + count, count)] = second_ref[...]

        row = lax.broadcasted_iota(jnp.int32, (tokens, ROWS, head_dim), 1) + j * ROWS
        new = jnp.swapaxes(placed[pl.ds(pl.multiple_of(j * ROWS, ROWS), ROWS)], 0, 1)
        keep = jnp.logical_or(row < low, row >= low + mine)
        out_ref[...] = jnp.where(keep, old_ref[...], new)

    piece = pl.BlockSpec((count, tokens, head_dim), lambda j, s: (0, 0, 0))
    return pl.pallas_call(
        kernel,
        grid_spec=pltpu.PrefetchScalarGridSpec(
            num_scalar_prefetch=1,
            grid=(window // ROWS,),
            in_specs=[
                piece,
                piece,
                pl.BlockSpec((tokens, ROWS, head_dim), lambda j, s: (0, j, 0)),
                pl.BlockSpec(memory_space=pl.ANY),
            ],
            out_specs=pl.BlockSpec((tokens, ROWS, head_dim), lambda j, s: (0, (s[0] * mine) // ROWS + j, 0)),
            scratch_shapes=[pltpu.VMEM((window, tokens, head_dim), jnp.bfloat16)],
        ),
        out_shape=jax.ShapeDtypeStruct(gathered.shape, gathered.dtype),
        input_output_aliases={4: 0},
        compiler_params=PARAMS,
        name="complete",
    )(slot, *pieces, old, gathered)


def across(value, route):
    return lax.ppermute(value, "section", route)


def rows_of(array):
    return array.reshape(-1, array.shape[-1])


def after(values, others):
    return lax.optimization_barrier((values, others))[0]


def square_body(queries, keys_values, positions, documents):
    mine = keys_values.shape[2]
    half = mine // 2
    section = lax.axis_index("section")
    beside_x, beside_y, opposite = section ^ 1, section ^ 2, section ^ 3
    tokens = documents.shape[0]
    share, share_a, share_b, cosine, sine = prepare_cache(keys_values, positions, documents)
    cache_a = across(share_a, ACROSS_X)
    cache_b = across(share_b, ACROSS_Y)
    before = shifted(share, "ctx")

    starts = jnp.stack(
        [
            beside_y * mine,
            beside_x * mine + half,
            opposite * mine,
            opposite * mine + half,
            section * mine,
            beside_x * mine,
            beside_y * mine + half,
        ]
    ).astype(jnp.int32)
    near_y, near_x, far_y, far_x, own_near, own_far = prepare_queries(
        queries[0], cosine, sine, starts, ((half,), (half,), (half,), (half,), (mine,), (half, half))
    )
    near_a = across(near_y, ACROSS_Y)
    near_b = across(near_x, ACROSS_X)
    cache_a, cache_b = after((cache_a, cache_b), (near_y, before))
    earlier_a = shifted(cache_a, "ctx")
    earlier_b = shifted(cache_b, "ctx")
    far_a = across(far_y, ACROSS_Y)
    far_b = across(far_x, ACROSS_X)

    blocks = tokens // BLOCK
    ids = before[2 * mine].astype(jnp.int32)
    share, before = rows_of(share), rows_of(before)
    earlier_docs = ids[:blocks] * ID_BASE + ids[blocks : 2 * blocks]
    earlier_docs = jnp.where(lax.axis_index("ctx") == 0, -1, earlier_docs)
    near = (((share, 0, mine), (before, 0, mine)), ((share, half, mine), (before, half, mine)))
    out_near_a, out_near_b = attend(
        (((near_a, 0, half), *near[0]), ((near_b, 0, half), *near[1])), documents, earlier_docs, 5 * 10**10
    )
    back_near_a = across(out_near_a, ACROSS_Y)
    back_near_b = across(after(out_near_b, earlier_a), ACROSS_X)
    own_near = after(own_near, out_near_a)
    own_near_a, own_near_b = attend(
        (((own_near, 0, half), *near[0]), ((own_near, half, half), *near[1])), documents, earlier_docs
    )
    far_a, earlier_a = after((far_a, earlier_a), own_near_a)
    far_of_a = tuple((rows_of(c), 0, half) for c in (cache_a, earlier_a))
    (out_far_a,) = attend((((far_a, 0, half), *far_of_a),), documents, earlier_docs)
    back_far_a = across(out_far_a, ACROSS_Y)
    far_b, earlier_b = after((far_b, earlier_b), out_far_a)
    far_of_b = tuple((rows_of(c), 0, half) for c in (cache_b, earlier_b))
    (out_far_b,) = attend((((far_b, 0, half), *far_of_b),), documents, earlier_docs)
    back_far_b = across(out_far_b, ACROSS_X)
    own_far = after(own_far, out_far_b)
    own_far_a, own_far_b = attend(
        (((own_far, 0, half), *far_of_a), ((own_far, half, half), *far_of_b)), documents, earlier_docs
    )

    slots = jnp.stack(
        [2 * section, 2 * section + 1, 2 * beside_x, 2 * beside_y + 1, 2 * beside_y, 2 * beside_x + 1]
    ).astype(jnp.int32)
    pieces = (own_near_a, own_near_b, own_far_a, own_far_b, back_near_a, back_near_b)
    start = (opposite * mine) // ROWS
    window = -(-mine // ROWS) * ROWS
    gathered, old = assemble(pieces, slots, queries.shape[2], start.astype(jnp.int32), window)
    back_far_a = after(back_far_a, gathered)
    back_far_b = after(back_far_b, back_far_a)
    return complete(gathered, old, (back_far_a, back_far_b), opposite[None].astype(jnp.int32))[None]


def general_body(queries, keys_values, positions, documents):
    heads = queries.shape[2]
    mine = keys_values.shape[2]
    earlier_docs = shifted(documents, "ctx")
    earlier_docs = jnp.where(lax.axis_index("ctx") == 0, -1, earlier_docs)
    share, _, _, cosine, sine = prepare_cache(keys_values, positions, documents)
    share = share[:-1].reshape(2, mine, *share.shape[1:])
    whole = lax.all_gather(share, "section", axis=1, tiled=True)
    earlier = shifted(whole, "ctx")
    starts = jnp.zeros((1,), jnp.int32)
    (rotated,) = prepare_queries(queries[0], cosine, sine, starts, ((heads,),))
    outs = []
    for first in range(0, heads, mine):
        chunk = slice(first, first + mine)
        caches = ((rows_of(c[:, chunk]), 0, mine) for c in (whole, earlier))
        group = ((rotated[chunk], 0, mine), *caches)
        outs += attend((group,), documents, earlier_docs)
    return assemble(outs, jnp.arange(len(outs), dtype=jnp.int32), heads)[0][None]


def solution(mesh):
    placed = (P("section", "ctx", None, None), P("ctx", None, "section", None), P("ctx"), P("ctx"))
    body = square_body if mesh.shape["section"] == 4 else general_body
    return jax.shard_map(
        body, mesh=mesh, in_specs=placed, out_specs=P("section", "ctx", None, None), check_vma=False
    )
```

```python
import functools

import jax
import jax.numpy as jnp
import numpy as np
from jax import lax
from jax.experimental import pallas as pl
from jax.experimental.pallas import tpu as pltpu
from jax.sharding import PartitionSpec as P

ACROSS_X = ((0, 1), (1, 0), (2, 3), (3, 2))
ACROSS_Y = ((0, 2), (2, 0), (1, 3), (3, 1))
BLOCK = 128
ROWS = 8
PARAMS = pltpu.CompilerParams(vmem_limit_bytes=12 * 2**20)
IN_VMEM = pl.BlockSpec(memory_space=pltpu.VMEM)
IN_SMEM = pl.BlockSpec(memory_space=pltpu.SMEM)
NT = (((1,), (1,)), ((), ()))


def shifted(block, axis):
    size = lax.axis_size(axis)
    return lax.ppermute(block, axis, [(i, (i + 1) % size) for i in range(size)])


def turn(values, cosine, sine):
    return (values * cosine + pltpu.roll(values, values.shape[-1] // 2, 1) * sine).astype(jnp.bfloat16)


def prepare_cache(raws, positions=None, tables=None):
    tokens, head_dim = raws[0].shape[0], raws[0].shape[-1]
    half_dim = head_dim // 2
    steps = tokens // BLOCK
    counts = [raw.shape[2] for raw in raws]
    rows = [jnp.transpose(raw, (0, 2, 1, 3)).reshape(-1, head_dim) for raw in raws]
    exponent = np.arange(half_dim, dtype=np.float32) * np.float32(2.0 / head_dim)
    inverse = np.power(np.float32(10000.0), -exponent).astype(np.float32)
    inverse = jnp.asarray(np.concatenate([inverse, inverse])[None])

    def fill_tables(positions_ref, inverse_ref, cosine_ref, sine_ref):
        left = lax.broadcasted_iota(jnp.int32, (BLOCK, head_dim), 1) < half_dim
        columns = [
            jnp.transpose(jnp.broadcast_to(positions_ref[i : i + 1], (BLOCK, BLOCK))).astype(jnp.float32)
            for i in range(steps)
        ]
        for i in range(0, steps, 2):
            other = min(i + 1, steps - 1)
            angles = jnp.where(left, columns[i], columns[other]) * inverse_ref[...]
            cosine, sine = jnp.cos(angles), jnp.sin(angles)
            turned_cosine, turned_sine = (pltpu.roll(t, half_dim, 1) for t in (cosine, sine))
            for k, (c, s) in enumerate(
                (
                    (jnp.where(left, cosine, turned_cosine), jnp.where(left, -sine, turned_sine)),
                    (jnp.where(left, turned_cosine, cosine), jnp.where(left, -turned_sine, sine)),
                )
            ):
                if i + k < steps:
                    at = slice((i + k) * BLOCK, (i + k + 1) * BLOCK)
                    cosine_ref[at] = c
                    sine_ref[at] = s

    def kernel(*refs):
        *refs, wide = refs
        row_refs, refs = refs[: len(rows)], refs[len(rows) :]
        (first, second), out_refs = refs[:2], refs[2 : 2 + len(rows)]
        if tables is None:
            cosine_ref, sine_ref = refs[-2:]
            fill_tables(first, second, cosine_ref, sine_ref)
        else:
            cosine_ref, sine_ref = first, second
        for heads, row_ref, out_ref in zip(counts, row_refs, out_refs):
            wide[: 2 * heads * tokens] = row_ref[...].astype(jnp.float32)
            for head in range(heads):
                key = wide[pl.ds(2 * head, tokens, stride=2 * heads), :]
                out_ref[0, head] = turn(key, cosine_ref[...], sine_ref[...])
                value = wide[pl.ds(2 * head + 1, tokens, stride=2 * heads), :]
                out_ref[1, head] = value.astype(jnp.bfloat16)

    out_shape = [jax.ShapeDtypeStruct((2, n, tokens, head_dim), jnp.bfloat16) for n in counts]
    if tables is None:
        out_shape += [jax.ShapeDtypeStruct((tokens, head_dim), jnp.float32)] * 2
    return pl.pallas_call(
        kernel,
        in_specs=[IN_VMEM] * (len(rows) + 2),
        out_specs=[IN_VMEM] * len(out_shape),
        out_shape=out_shape,
        scratch_shapes=[pltpu.VMEM((2 * max(counts) * tokens, head_dim), jnp.float32)],
        compiler_params=PARAMS,
        cost_estimate=pl.CostEstimate(flops=1, bytes_accessed=1, transcendentals=0),
        name="prepare_cache",
    )(*rows, *((positions.reshape(steps, BLOCK), inverse) if tables is None else tables))


def prepare_queries(queries, cosine, sine, starts, counts):
    tokens, heads, head_dim = queries.shape

    def kernel(starts_ref, queries_ref, cosine_ref, sine_ref, *refs):
        wide = refs[-1]
        wide[...] = queries_ref[...].reshape(tokens * heads, head_dim).astype(jnp.float32)
        run = 0
        for out_ref, runs in zip(refs[:-1], counts):
            slot = 0
            for count in runs:
                for i in range(count):
                    head = wide[pl.ds(starts_ref[run] + i, tokens, stride=heads), :]
                    out_ref[slot] = turn(head, cosine_ref[...], sine_ref[...])
                    slot += 1
                run += 1

    totals = [sum(runs) for runs in counts]
    return pl.pallas_call(
        kernel,
        in_specs=[IN_SMEM] + [IN_VMEM] * 3,
        out_specs=[IN_VMEM] * len(totals),
        out_shape=[jax.ShapeDtypeStruct((n, tokens, head_dim), jnp.bfloat16) for n in totals],
        scratch_shapes=[pltpu.VMEM((tokens * heads, head_dim), jnp.float32)],
        compiler_params=PARAMS,
        cost_estimate=pl.CostEstimate(
            flops=2 * 10**9, bytes_accessed=4 * queries.size, transcendentals=0
        ),
        name="prepare_queries",
    )(starts, queries, cosine, sine)


def attend(sets, documents, earlier_docs, flops=1):
    count = sets[0][0][2]
    tokens, head_dim = sets[0][0][0].shape[-2:]
    blocks = tokens // BLOCK
    width = tokens + BLOCK
    scale = float(head_dim**-0.5 * np.log2(np.e))
    n = len(sets)

    def kernel(docs_ref, earlier_ref, *refs):
        bias = refs[-1]
        window = [earlier_ref[i : i + 1] for i in range(blocks)] + [docs_ref[i : i + 1] for i in range(blocks)]
        row = lax.broadcasted_iota(jnp.int32, (BLOCK, BLOCK), 0)
        column = lax.broadcasted_iota(jnp.int32, (BLOCK, BLOCK), 1)
        for r in range(blocks):
            mine = jnp.transpose(jnp.broadcast_to(docs_ref[r : r + 1], (BLOCK, BLOCK)))
            for c in range(blocks + 1):
                allowed = window[r + c] == mine
                if c == blocks:
                    allowed = jnp.logical_and(allowed, column <= row)
                bias[r, :, c * BLOCK : (c + 1) * BLOCK] = jnp.where(allowed, 0.0, -1e30)
        for head in range(count):
            for g, group in enumerate(sets):
                q, c, e = refs[3 * g : 3 * g + 3]
                q_head = group[0][1] + head

                def band(kind, low, high):
                    (_, c_first, c_heads), (_, e_first, e_heads) = group[1:]
                    c_row = (kind * c_heads + c_first + head) * tokens
                    e_row = (kind * e_heads + e_first + head) * tokens
                    return jnp.concatenate([e[e_row + low : e_row + tokens], c[c_row : c_row + high]], axis=0)

                for r in range(blocks):
                    low, high = BLOCK * r, BLOCK * (r + 1)
                    key, value = band(0, low, high), band(1, low, high)
                    scores = lax.dot_general(q[q_head, low:high], key, NT, preferred_element_type=jnp.float32)
                    scores = scores + bias[r]
                    largest = jnp.max(scores, axis=1, keepdims=True) * scale
                    weights = jnp.exp2(scores * scale - largest).astype(jnp.bfloat16)
                    extended = jnp.concatenate([value, jnp.ones_like(value)], axis=1)
                    mixed = jnp.dot(weights, extended, preferred_element_type=jnp.float32)
                    mixed = (mixed[:, :head_dim] / mixed[:, head_dim:]).astype(jnp.bfloat16)
                    refs[3 * n + g][head, low:high] = mixed

    return pl.pallas_call(
        kernel,
        in_specs=[IN_VMEM] * (2 + 3 * n),
        out_specs=[IN_VMEM] * n,
        out_shape=[jax.ShapeDtypeStruct((count, tokens, head_dim), jnp.bfloat16)] * n,
        scratch_shapes=[pltpu.VMEM((blocks, BLOCK, width), jnp.float32)],
        compiler_params=PARAMS,
        cost_estimate=pl.CostEstimate(flops=flops, bytes_accessed=1, transcendentals=0),
        name="attend",
    )(documents.reshape(blocks, BLOCK), earlier_docs.reshape(blocks, BLOCK), *[o[0] for group in sets for o in group])


def assemble(pieces, slots, heads, window_start=None, window=0):
    count, tokens, head_dim = pieces[0].shape
    step = BLOCK

    def kernel(slots_ref, *refs):
        piece_refs, outs, gathered = refs[: len(pieces)], refs[len(pieces) : -1], refs[-1]
        for p, ref in enumerate(piece_refs):
            gathered[pl.ds(slots_ref[p] * count, count)] = ref[...]
        outs[0][...] = jnp.swapaxes(gathered[...], 0, 1)
        if window:
            first = pl.multiple_of(slots_ref[len(pieces)] * ROWS, ROWS)
            outs[1][...] = gathered[pl.ds(first, window)]

    if window:
        slots = jnp.concatenate([slots, window_start[None]])
    out_specs = [pl.BlockSpec((step, heads, head_dim), lambda i, s: (i, 0, 0))]
    out_shape = [jax.ShapeDtypeStruct((tokens, heads, head_dim), jnp.bfloat16)]
    if window:
        out_specs.append(pl.BlockSpec((window, step, head_dim), lambda i, s: (0, i, 0)))
        out_shape.append(jax.ShapeDtypeStruct((window, tokens, head_dim), jnp.bfloat16))
    return pl.pallas_call(
        kernel,
        grid_spec=pltpu.PrefetchScalarGridSpec(
            num_scalar_prefetch=1,
            grid=(tokens // step,),
            in_specs=[pl.BlockSpec((count, step, head_dim), lambda i, s: (0, i, 0))] * len(pieces),
            out_specs=out_specs,
            scratch_shapes=[pltpu.VMEM((heads, step, head_dim), jnp.bfloat16)],
        ),
        out_shape=out_shape,
        compiler_params=PARAMS,
        cost_estimate=pl.CostEstimate(flops=10**9, bytes_accessed=1, transcendentals=0),
        name="assemble",
    )(slots, *pieces)


def complete(gathered, old, pieces, slot):
    count, tokens, head_dim = pieces[0].shape
    mine = 2 * count
    window = old.shape[0]

    steps = tokens // BLOCK

    def kernel(slot_ref, first_ref, second_ref, old_ref, _, out_ref, placed, ready, sems):
        block = (slot_ref[0] * mine) // ROWS
        low = slot_ref[0] * mine - block * ROWS
        placed[...] = old_ref[...]
        placed[pl.ds(low, count)] = first_ref[...]
        placed[pl.ds(low + count, count)] = second_ref[...]
        heads_at = pl.ds(pl.multiple_of(block * ROWS, ROWS), window)
        copies = []
        for i in range(steps):
            at = slice(i * BLOCK, (i + 1) * BLOCK)
            ready[at] = jnp.swapaxes(placed[:, at], 0, 1)
            at = pl.ds(i * BLOCK, BLOCK)
            copies.append(pltpu.make_async_copy(ready.at[at], out_ref.at[at, heads_at], sems.at[i]))
            copies[i].start()
        for copy in copies:
            copy.wait()

    anywhere = pl.BlockSpec(memory_space=pl.ANY)
    return pl.pallas_call(
        kernel,
        in_specs=[IN_SMEM, IN_VMEM, IN_VMEM, IN_VMEM, anywhere],
        out_specs=anywhere,
        out_shape=jax.ShapeDtypeStruct(gathered.shape, gathered.dtype),
        scratch_shapes=[
            pltpu.VMEM((window, tokens, head_dim), jnp.bfloat16),
            pltpu.VMEM((tokens, window, head_dim), jnp.bfloat16),
            pltpu.SemaphoreType.DMA((steps,)),
        ],
        input_output_aliases={4: 0},
        compiler_params=PARAMS,
        name="complete",
    )(slot, *pieces, old, gathered)


def across(value, route):
    return lax.ppermute(value, "section", route)


def rows_of(array):
    return array.reshape(-1, array.shape[-1])


def after(values, others):
    return lax.optimization_barrier((values, others))[0]


def square_body(queries, keys_values, positions, documents):
    mine = keys_values.shape[2]
    half = mine // 2
    section = lax.axis_index("section")
    beside_x, beside_y, opposite = section ^ 1, section ^ 2, section ^ 3
    part_a, part_b = keys_values[:, :, :half], keys_values[:, :, half:]
    raw_a = across(part_a, ACROSS_X)
    raw_b = across(part_b, ACROSS_Y)
    raw_before = shifted(keys_values, "ctx")
    labels = shifted(jnp.stack([positions, documents]), "ctx")
    share, cosine, sine = prepare_cache((keys_values,), positions)

    starts = jnp.stack(
        [
            beside_y * mine,
            beside_x * mine + half,
            opposite * mine,
            opposite * mine + half,
            section * mine,
            beside_x * mine,
            beside_y * mine + half,
        ]
    ).astype(jnp.int32)
    near_y, near_x, far_y, far_x, own_near, own_far = prepare_queries(
        queries[0], cosine, sine, starts, ((half,), (half,), (half,), (half,), (mine,), (half, half))
    )
    near_a = across(near_y, ACROSS_Y)
    near_b = across(near_x, ACROSS_X)
    raw_a, raw_b = after((raw_a, raw_b), (near_y, raw_before))
    raw_earlier_a = shifted(raw_a, "ctx")
    raw_earlier_b = shifted(after(raw_b, near_a), "ctx")
    far_a = across(far_y, ACROSS_Y)
    far_b = across(far_x, ACROSS_X)

    before, *earlier_tables = prepare_cache((raw_before,), labels[0])
    earlier_docs = jnp.where(lax.axis_index("ctx") == 0, -1, labels[1])
    cache_a, cache_b = prepare_cache((raw_a, raw_b), tables=(cosine, sine))
    near_a, near_b = after((near_a, near_b), (before, cache_a))
    share, before = rows_of(share), rows_of(before)
    near = (((share, 0, mine), (before, 0, mine)), ((share, half, mine), (before, half, mine)))
    out_near_a, out_near_b = attend(
        (((near_a, 0, half), *near[0]), ((near_b, 0, half), *near[1])), documents, earlier_docs, 5 * 10**10
    )
    back_near_a = across(out_near_a, ACROSS_Y)
    back_near_b = across(after(out_near_b, raw_earlier_a), ACROSS_X)
    own_near = after(own_near, out_near_a)
    own_near_a, own_near_b = attend(
        (((own_near, 0, half), *near[0]), ((own_near, half, half), *near[1])), documents, earlier_docs
    )
    far_a, raw_earlier_a = after((far_a, raw_earlier_a), own_near_a)
    (earlier_a,) = prepare_cache((raw_earlier_a,), tables=earlier_tables)
    far_of_a = tuple((rows_of(c), 0, half) for c in (cache_a, earlier_a))
    (out_far_a,) = attend((((far_a, 0, half), *far_of_a),), documents, earlier_docs)
    back_far_a = across(out_far_a, ACROSS_Y)
    far_b, raw_earlier_b = after((far_b, raw_earlier_b), out_far_a)
    (earlier_b,) = prepare_cache((raw_earlier_b,), tables=earlier_tables)
    far_of_b = tuple((rows_of(c), 0, half) for c in (cache_b, earlier_b))
    (out_far_b,) = attend((((far_b, 0, half), *far_of_b),), documents, earlier_docs)
    back_far_b = across(out_far_b, ACROSS_X)
    own_far = after(own_far, out_far_b)
    own_far_a, own_far_b = attend(
        (((own_far, 0, half), *far_of_a), ((own_far, half, half), *far_of_b)), documents, earlier_docs
    )

    slots = jnp.stack(
        [2 * section, 2 * section + 1, 2 * beside_x, 2 * beside_y + 1, 2 * beside_y, 2 * beside_x + 1]
    ).astype(jnp.int32)
    pieces = (own_near_a, own_near_b, own_far_a, own_far_b, back_near_a, back_near_b)
    start = (opposite * mine) // ROWS
    window = -(-mine // ROWS) * ROWS
    gathered, old = assemble(pieces, slots, queries.shape[2], start.astype(jnp.int32), window)
    back_far_a = after(back_far_a, gathered)
    back_far_b = after(back_far_b, back_far_a)
    return complete(gathered, old, (back_far_a, back_far_b), opposite[None].astype(jnp.int32))[None]


def general_body(queries, keys_values, positions, documents):
    heads = queries.shape[2]
    mine = keys_values.shape[2]
    earlier_docs = shifted(documents, "ctx")
    earlier_docs = jnp.where(lax.axis_index("ctx") == 0, -1, earlier_docs)
    share, cosine, sine = prepare_cache((keys_values,), positions)
    whole = lax.all_gather(share, "section", axis=1, tiled=True)
    earlier = shifted(whole, "ctx")
    starts = jnp.zeros((1,), jnp.int32)
    (rotated,) = prepare_queries(queries[0], cosine, sine, starts, ((heads,),))
    outs = []
    for first in range(0, heads, mine):
        chunk = slice(first, first + mine)
        caches = ((rows_of(c[:, chunk]), 0, mine) for c in (whole, earlier))
        group = ((rotated[chunk], 0, mine), *caches)
        outs += attend((group,), documents, earlier_docs)
    return assemble(outs, jnp.arange(len(outs), dtype=jnp.int32), heads)[0][None]


def solution(mesh):
    placed = (P("section", "ctx", None, None), P("ctx", None, "section", None), P("ctx"), P("ctx"))
    body = square_body if mesh.shape["section"] == 4 else general_body
    return jax.shard_map(
        body, mesh=mesh, in_specs=placed, out_specs=P("section", "ctx", None, None), check_vma=False
    )
```

```python
import functools

import jax
import jax.numpy as jnp
import numpy as np
from jax import lax
from jax.experimental import pallas as pl
from jax.experimental.pallas import tpu as pltpu
from jax.sharding import PartitionSpec as P

ACROSS_X = ((0, 1), (1, 0), (2, 3), (3, 2))
ACROSS_Y = ((0, 2), (2, 0), (1, 3), (3, 1))
BLOCK = 128
ROWS = 8
PARAMS = pltpu.CompilerParams(vmem_limit_bytes=12 * 2**20)
IN_VMEM = pl.BlockSpec(memory_space=pltpu.VMEM)
IN_SMEM = pl.BlockSpec(memory_space=pltpu.SMEM)
NT = (((1,), (1,)), ((), ()))


def shifted(block, axis):
    size = lax.axis_size(axis)
    return lax.ppermute(block, axis, [(i, (i + 1) % size) for i in range(size)])


def turn(values, cosine, sine):
    return (values * cosine + pltpu.roll(values, values.shape[-1] // 2, 1) * sine).astype(jnp.bfloat16)


def prepare_cache(raws, positions=None, tables=None):
    tokens, head_dim = raws[0].shape[0], raws[0].shape[-1]
    half_dim = head_dim // 2
    steps = tokens // BLOCK
    counts = [raw.shape[2] for raw in raws]
    rows = [jnp.transpose(raw, (0, 2, 1, 3)).reshape(-1, head_dim) for raw in raws]
    exponent = np.arange(half_dim, dtype=np.float32) * np.float32(2.0 / head_dim)
    inverse = np.power(np.float32(10000.0), -exponent).astype(np.float32)
    inverse = jnp.asarray(np.concatenate([inverse, inverse])[None])

    def fill_tables(positions_ref, inverse_ref, cosine_ref, sine_ref):
        left = lax.broadcasted_iota(jnp.int32, (BLOCK, head_dim), 1) < half_dim
        columns = [
            jnp.transpose(jnp.broadcast_to(positions_ref[i : i + 1], (BLOCK, BLOCK))).astype(jnp.float32)
            for i in range(steps)
        ]
        for i in range(0, steps, 2):
            other = min(i + 1, steps - 1)
            angles = jnp.where(left, columns[i], columns[other]) * inverse_ref[...]
            cosine, sine = jnp.cos(angles), jnp.sin(angles)
            turned_cosine, turned_sine = (pltpu.roll(t, half_dim, 1) for t in (cosine, sine))
            for k, (c, s) in enumerate(
                (
                    (jnp.where(left, cosine, turned_cosine), jnp.where(left, -sine, turned_sine)),
                    (jnp.where(left, turned_cosine, cosine), jnp.where(left, -turned_sine, sine)),
                )
            ):
                if i + k < steps:
                    at = slice((i + k) * BLOCK, (i + k + 1) * BLOCK)
                    cosine_ref[at] = c
                    sine_ref[at] = s

    def kernel(*refs):
        *refs, wide = refs
        row_refs, refs = refs[: len(rows)], refs[len(rows) :]
        (first, second), out_refs = refs[:2], refs[2 : 2 + len(rows)]
        if tables is None:
            cosine_ref, sine_ref = refs[-2:]
            fill_tables(first, second, cosine_ref, sine_ref)
        else:
            cosine_ref, sine_ref = first, second
        for heads, row_ref, out_ref in zip(counts, row_refs, out_refs):
            wide[: 2 * heads * tokens] = row_ref[...].astype(jnp.float32)
            for head in range(heads):
                key = wide[pl.ds(2 * head, tokens, stride=2 * heads), :]
                out_ref[0, head] = turn(key, cosine_ref[...], sine_ref[...])
                value = wide[pl.ds(2 * head + 1, tokens, stride=2 * heads), :]
                out_ref[1, head] = value.astype(jnp.bfloat16)

    out_shape = [jax.ShapeDtypeStruct((2, n, tokens, head_dim), jnp.bfloat16) for n in counts]
    if tables is None:
        out_shape += [jax.ShapeDtypeStruct((tokens, head_dim), jnp.float32)] * 2
    return pl.pallas_call(
        kernel,
        in_specs=[IN_VMEM] * (len(rows) + 2),
        out_specs=[IN_VMEM] * len(out_shape),
        out_shape=out_shape,
        scratch_shapes=[pltpu.VMEM((2 * max(counts) * tokens, head_dim), jnp.float32)],
        compiler_params=PARAMS,
        cost_estimate=pl.CostEstimate(flops=1, bytes_accessed=1, transcendentals=0),
        name="prepare_cache",
    )(*rows, *((positions.reshape(steps, BLOCK), inverse) if tables is None else tables))


def prepare_queries(queries, cosine, sine, starts, counts):
    tokens, heads, head_dim = queries.shape

    def kernel(starts_ref, queries_ref, cosine_ref, sine_ref, *refs):
        wide = refs[-1]
        wide[...] = queries_ref[...].reshape(tokens * heads, head_dim).astype(jnp.float32)
        run = 0
        for out_ref, runs in zip(refs[:-1], counts):
            slot = 0
            for count in runs:
                for i in range(count):
                    head = wide[pl.ds(starts_ref[run] + i, tokens, stride=heads), :]
                    out_ref[slot] = turn(head, cosine_ref[...], sine_ref[...])
                    slot += 1
                run += 1

    totals = [sum(runs) for runs in counts]
    return pl.pallas_call(
        kernel,
        in_specs=[IN_SMEM] + [IN_VMEM] * 3,
        out_specs=[IN_VMEM] * len(totals),
        out_shape=[jax.ShapeDtypeStruct((n, tokens, head_dim), jnp.bfloat16) for n in totals],
        scratch_shapes=[pltpu.VMEM((tokens * heads, head_dim), jnp.float32)],
        compiler_params=PARAMS,
        cost_estimate=pl.CostEstimate(
            flops=2 * 10**9, bytes_accessed=4 * queries.size, transcendentals=0
        ),
        name="prepare_queries",
    )(starts, queries, cosine, sine)


def attend(sets, documents, earlier_docs, flops=1):
    count = sets[0][0][2]
    tokens, head_dim = sets[0][0][0].shape[-2:]
    blocks = tokens // BLOCK
    width = tokens + BLOCK
    scale = float(head_dim**-0.5 * np.log2(np.e))
    n = len(sets)

    def kernel(docs_ref, earlier_ref, *refs):
        bias = refs[-1]
        window = [earlier_ref[i : i + 1] for i in range(blocks)] + [docs_ref[i : i + 1] for i in range(blocks)]
        row = lax.broadcasted_iota(jnp.int32, (BLOCK, BLOCK), 0)
        column = lax.broadcasted_iota(jnp.int32, (BLOCK, BLOCK), 1)
        for r in range(blocks):
            mine = jnp.transpose(jnp.broadcast_to(docs_ref[r : r + 1], (BLOCK, BLOCK)))
            for c in range(blocks + 1):
                allowed = window[r + c] == mine
                if c == blocks:
                    allowed = jnp.logical_and(allowed, column <= row)
                bias[r, :, c * BLOCK : (c + 1) * BLOCK] = jnp.where(allowed, 0.0, -1e30)
        for head in range(count):
            for g, group in enumerate(sets):
                q, c, e = refs[3 * g : 3 * g + 3]
                q_head = group[0][1] + head

                def band(kind, low, high):
                    (_, c_first, c_heads), (_, e_first, e_heads) = group[1:]
                    c_row = (kind * c_heads + c_first + head) * tokens
                    e_row = (kind * e_heads + e_first + head) * tokens
                    return jnp.concatenate([e[e_row + low : e_row + tokens], c[c_row : c_row + high]], axis=0)

                for r in range(blocks):
                    low, high = BLOCK * r, BLOCK * (r + 1)
                    key, value = band(0, low, high), band(1, low, high)
                    scores = lax.dot_general(q[q_head, low:high], key, NT, preferred_element_type=jnp.float32)
                    scores = scores + bias[r]
                    largest = jnp.max(scores, axis=1, keepdims=True) * scale
                    weights = jnp.exp2(scores * scale - largest).astype(jnp.bfloat16)
                    extended = jnp.concatenate([value, jnp.ones_like(value)], axis=1)
                    mixed = jnp.dot(weights, extended, preferred_element_type=jnp.float32)
                    mixed = (mixed[:, :head_dim] / mixed[:, head_dim:]).astype(jnp.bfloat16)
                    refs[3 * n + g][head, low:high] = mixed

    return pl.pallas_call(
        kernel,
        in_specs=[IN_VMEM] * (2 + 3 * n),
        out_specs=[IN_VMEM] * n,
        out_shape=[jax.ShapeDtypeStruct((count, tokens, head_dim), jnp.bfloat16)] * n,
        scratch_shapes=[pltpu.VMEM((blocks, BLOCK, width), jnp.float32)],
        compiler_params=PARAMS,
        cost_estimate=pl.CostEstimate(flops=flops, bytes_accessed=1, transcendentals=0),
        name="attend",
    )(documents.reshape(blocks, BLOCK), earlier_docs.reshape(blocks, BLOCK), *[o[0] for group in sets for o in group])


def assemble(pieces, slots, heads, window_start=None, window=0):
    count, tokens, head_dim = pieces[0].shape
    step = BLOCK

    def kernel(slots_ref, *refs):
        piece_refs, outs, gathered = refs[: len(pieces)], refs[len(pieces) : -1], refs[-1]
        for p, ref in enumerate(piece_refs):
            gathered[pl.ds(slots_ref[p] * count, count)] = ref[...]
        outs[0][...] = jnp.swapaxes(gathered[...], 0, 1)
        if window:
            first = pl.multiple_of(slots_ref[len(pieces)] * ROWS, ROWS)
            outs[1][...] = gathered[pl.ds(first, window)]

    if window:
        slots = jnp.concatenate([slots, window_start[None]])
    out_specs = [pl.BlockSpec((step, heads, head_dim), lambda i, s: (i, 0, 0))]
    out_shape = [jax.ShapeDtypeStruct((tokens, heads, head_dim), jnp.bfloat16)]
    if window:
        out_specs.append(pl.BlockSpec((window, step, head_dim), lambda i, s: (0, i, 0)))
        out_shape.append(jax.ShapeDtypeStruct((window, tokens, head_dim), jnp.bfloat16))
    return pl.pallas_call(
        kernel,
        grid_spec=pltpu.PrefetchScalarGridSpec(
            num_scalar_prefetch=1,
            grid=(tokens // step,),
            in_specs=[pl.BlockSpec((count, step, head_dim), lambda i, s: (0, i, 0))] * len(pieces),
            out_specs=out_specs,
            scratch_shapes=[pltpu.VMEM((heads, step, head_dim), jnp.bfloat16)],
        ),
        out_shape=out_shape,
        compiler_params=PARAMS,
        cost_estimate=pl.CostEstimate(flops=10**9, bytes_accessed=1, transcendentals=0),
        name="assemble",
    )(slots, *pieces)


def complete(gathered, old, pieces):
    count, tokens, head_dim = pieces[0].shape
    mine = 2 * count
    window = old.shape[0]

    steps = tokens // BLOCK

    def kernel(first_ref, second_ref, old_ref, _, out_ref, landed, placed, ready, load_sems, sems):
        loads = []
        for i in range(steps):
            at = pl.ds(i * BLOCK, BLOCK)
            loads.append(pltpu.make_async_copy(second_ref.at[:, at], landed.at[i], load_sems.at[i]))
            loads[i].start()
        first_head = (lax.axis_index("section") ^ 3) * mine
        block = first_head // ROWS
        low = first_head - block * ROWS
        placed[...] = old_ref[...]
        placed[pl.ds(low, count)] = first_ref[...]
        heads_at = pl.ds(pl.multiple_of(block * ROWS, ROWS), window)
        copies = []
        for i in range(steps):
            at = slice(i * BLOCK, (i + 1) * BLOCK)
            loads[i].wait()
            placed[pl.ds(low + count, count), at] = landed[i]
            ready[at] = jnp.swapaxes(placed[:, at], 0, 1)
            at = pl.ds(i * BLOCK, BLOCK)
            copies.append(pltpu.make_async_copy(ready.at[at], out_ref.at[at, heads_at], sems.at[i]))
            copies[i].start()
        for copy in copies:
            copy.wait()

    anywhere = pl.BlockSpec(memory_space=pl.ANY)
    return pl.pallas_call(
        kernel,
        in_specs=[IN_VMEM, anywhere, IN_VMEM, anywhere],
        out_specs=anywhere,
        out_shape=jax.ShapeDtypeStruct(gathered.shape, gathered.dtype),
        scratch_shapes=[
            pltpu.VMEM((steps, count, BLOCK, head_dim), jnp.bfloat16),
            pltpu.VMEM((window, tokens, head_dim), jnp.bfloat16),
            pltpu.VMEM((tokens, window, head_dim), jnp.bfloat16),
            pltpu.SemaphoreType.DMA((steps,)),
            pltpu.SemaphoreType.DMA((steps,)),
        ],
        input_output_aliases={3: 0},
        compiler_params=PARAMS,
        name="complete",
    )(*pieces, old, gathered)


def across(value, route):
    return lax.ppermute(value, "section", route)


def rows_of(array):
    return array.reshape(-1, array.shape[-1])


def after(values, others):
    return lax.optimization_barrier((values, others))[0]


def square_body(queries, keys_values, positions, documents):
    mine = keys_values.shape[2]
    half = mine // 2
    section = lax.axis_index("section")
    beside_x, beside_y, opposite = section ^ 1, section ^ 2, section ^ 3
    part_a, part_b = keys_values[:, :, :half], keys_values[:, :, half:]
    raw_a = across(part_a, ACROSS_X)
    raw_b = across(part_b, ACROSS_Y)
    raw_before = shifted(keys_values, "ctx")
    labels = shifted(jnp.stack([positions, documents]), "ctx")
    share, cosine, sine = prepare_cache((keys_values,), positions)

    starts = jnp.stack(
        [
            beside_y * mine,
            beside_x * mine + half,
            opposite * mine,
            opposite * mine + half,
            section * mine,
            beside_x * mine,
            beside_y * mine + half,
        ]
    ).astype(jnp.int32)
    near_y, near_x, far_y, far_x, own_near, own_far = prepare_queries(
        queries[0], cosine, sine, starts, ((half,), (half,), (half,), (half,), (mine,), (half, half))
    )
    near_a = across(near_y, ACROSS_Y)
    near_b = across(near_x, ACROSS_X)
    raw_a, raw_b = after((raw_a, raw_b), (near_y, raw_before))
    raw_earlier_a = shifted(raw_a, "ctx")
    raw_earlier_b = shifted(after(raw_b, near_a), "ctx")
    far_a = across(far_y, ACROSS_Y)
    far_b = across(far_x, ACROSS_X)

    before, *earlier_tables = prepare_cache((raw_before,), labels[0])
    earlier_docs = jnp.where(lax.axis_index("ctx") == 0, -1, labels[1])
    cache_a, cache_b = prepare_cache((raw_a, raw_b), tables=(cosine, sine))
    near_a, near_b = after((near_a, near_b), (before, cache_a))
    share, before = rows_of(share), rows_of(before)
    near = (((share, 0, mine), (before, 0, mine)), ((share, half, mine), (before, half, mine)))
    out_near_a, out_near_b = attend(
        (((near_a, 0, half), *near[0]), ((near_b, 0, half), *near[1])), documents, earlier_docs, 5 * 10**10
    )
    back_near_a = across(out_near_a, ACROSS_Y)
    back_near_b = across(after(out_near_b, raw_earlier_a), ACROSS_X)
    own_near = after(own_near, out_near_a)
    own_near_a, own_near_b = attend(
        (((own_near, 0, half), *near[0]), ((own_near, half, half), *near[1])), documents, earlier_docs
    )
    far_a, raw_earlier_a = after((far_a, raw_earlier_a), own_near_a)
    (earlier_a,) = prepare_cache((raw_earlier_a,), tables=earlier_tables)
    far_of_a = tuple((rows_of(c), 0, half) for c in (cache_a, earlier_a))
    (out_far_a,) = attend((((far_a, 0, half), *far_of_a),), documents, earlier_docs)
    back_far_a = across(out_far_a, ACROSS_Y)
    far_b, raw_earlier_b = after((far_b, raw_earlier_b), out_far_a)
    (earlier_b,) = prepare_cache((raw_earlier_b,), tables=earlier_tables)
    far_of_b = tuple((rows_of(c), 0, half) for c in (cache_b, earlier_b))
    (out_far_b,) = attend((((far_b, 0, half), *far_of_b),), documents, earlier_docs)
    back_far_b = across(out_far_b, ACROSS_X)
    own_far = after(own_far, out_far_b)
    own_far_a, own_far_b = attend(
        (((own_far, 0, half), *far_of_a), ((own_far, half, half), *far_of_b)), documents, earlier_docs
    )

    slots = jnp.stack(
        [2 * section, 2 * section + 1, 2 * beside_x, 2 * beside_y + 1, 2 * beside_y, 2 * beside_x + 1]
    ).astype(jnp.int32)
    pieces = (own_near_a, own_near_b, own_far_a, own_far_b, back_near_a, back_near_b)
    start = (opposite * mine) // ROWS
    window = -(-mine // ROWS) * ROWS
    gathered, old = assemble(pieces, slots, queries.shape[2], start.astype(jnp.int32), window)
    back_far_a = after(back_far_a, gathered)
    back_far_b = after(back_far_b, back_far_a)
    return complete(gathered, old, (back_far_a, back_far_b))[None]


def general_body(queries, keys_values, positions, documents):
    heads = queries.shape[2]
    mine = keys_values.shape[2]
    earlier_docs = shifted(documents, "ctx")
    earlier_docs = jnp.where(lax.axis_index("ctx") == 0, -1, earlier_docs)
    share, cosine, sine = prepare_cache((keys_values,), positions)
    whole = lax.all_gather(share, "section", axis=1, tiled=True)
    earlier = shifted(whole, "ctx")
    starts = jnp.zeros((1,), jnp.int32)
    (rotated,) = prepare_queries(queries[0], cosine, sine, starts, ((heads,),))
    outs = []
    for first in range(0, heads, mine):
        chunk = slice(first, first + mine)
        caches = ((rows_of(c[:, chunk]), 0, mine) for c in (whole, earlier))
        group = ((rotated[chunk], 0, mine), *caches)
        outs += attend((group,), documents, earlier_docs)
    return assemble(outs, jnp.arange(len(outs), dtype=jnp.int32), heads)[0][None]


def solution(mesh):
    placed = (P("section", "ctx", None, None), P("ctx", None, "section", None), P("ctx"), P("ctx"))
    body = square_body if mesh.shape["section"] == 4 else general_body
    return jax.shard_map(
        body, mesh=mesh, in_specs=placed, out_specs=P("section", "ctx", None, None), check_vma=False
    )
```
